32 devices in a mesh: grp: 2 (over x), tile: 16 (over z, y, core).
Axes of the slice: x: 2, y: 2, z: 4, core: 2. Of those that a mesh axis runs over, the one named last changes fastest.
Arguments:
- queries: bfloat16 [8192, 2560], P(('grp', 'tile')), parts along dimension 0, may hold values from -150 to 150
- key_vectors: bfloat16 [8192, 2560], P(('grp', 'tile')), parts along dimension 0, may hold values from -4 to 4
- value_vectors: bfloat16 [8192, 2560], P(('grp', 'tile')), parts along dimension 0, may hold values from -6 to 6
- query_tangent: bfloat16 [8192, 2560], P(('grp', 'tile')), parts along dimension 0, may hold values from -6 to 6
- key_tangent: bfloat16 [8192, 2560], P(('grp', 'tile')), parts along dimension 0, may hold values from -6 to 6
- value_tangent: bfloat16 [8192, 2560], P(('grp', 'tile')), parts along dimension 0, may hold values from -6 to 6
- key_tiles: int32 [32, 5], P(('grp', 'tile')), parts along dimension 0, may hold values from 0 to 15, as said below
- tile_counts: int32 [32], P(('grp', 'tile')), parts along dimension 0, may hold values from 1 to 5
Outputs:
- attended: bfloat16 [8192, 2560], P(('grp', 'tile')), parts along dimension 0
- attended_tangent: bfloat16 [8192, 2560], P(('grp', 'tile')), parts along dimension 0
The draws below stay inside these ranges and needn't reach their ends.
There are 2 independent parts, one for each index of `grp`. The reference program is written for one: setup_inputs(seed, part) draws one part's arguments, and reference() takes and returns one part's arrays. A program takes and returns all parts, laid end to end along the dimension named above; each array names one. Nothing has to cross between parts.
Inputs may be any that keep to these rules, and one draw needn't show every extreme that they name: `key_tiles`: row t begins with t; its first tile_counts[t] entries are distinct tiles at most 2 away from t; the later entries are tiles at most 2 away from t and carry no weight.
All inputs are finite; a program needn't handle non-finite values.
Results may differ from the reference program's by a relative error of at most 0.0048.
Values may be sent and summed in bfloat16 or wider, within the bound.
A program may use at most 128 MiB of HBM per device.

```python
import math
import jax
import jax.numpy as jnp
from jax import lax

HEADS = 20
D_HEAD = 128
TILE = 256
REACH = 2
SEL = 5
TILES = 16
TOKENS = 4096


def pair_draw(key):
    width = HEADS * D_HEAD
    query_draw = jax.random.truncated_normal(jax.random.fold_in(key, 11), -4.0, 4.0, (TOKENS, width), jnp.float32)
    key_draw = jax.random.truncated_normal(jax.random.fold_in(key, 12), -4.0, 4.0, (TOKENS, width), jnp.float32)
    return (query_draw, key_draw)


def draw_queries(key, part):
    return pair_draw(key)[0].astype(jnp.bfloat16)


def draw_key_vectors(key, part):
    return pair_draw(key)[1].astype(jnp.bfloat16)


def select_draw(key):
    tile_ids = jnp.arange(TILES)
    offsets = jnp.concatenate([jnp.arange(-REACH, 0), jnp.arange(1, REACH + 1)])
    candidate = tile_ids[:, None] + offsets[None, :]
    inside = (candidate >= 0) & (candidate < TILES)
    ranking_score = jax.random.randint(jax.random.fold_in(key, 21), (TILES, 2 * REACH), 0, 4096) * (2 * REACH) + jnp.arange(2 * REACH)[None, :] + jnp.where(inside, 0, 1 << 20)
    ranking = jnp.argsort(ranking_score, axis=1, stable=True)
    sorted_candidate = jnp.take_along_axis(candidate, ranking, axis=1)
    sorted_inside = jnp.take_along_axis(inside, ranking, axis=1)
    listed = jnp.where(sorted_inside, sorted_candidate, tile_ids[:, None])
    key_list = jnp.concatenate([tile_ids[:, None], listed], axis=1).astype(jnp.int32)
    inside_count = jnp.sum(inside.astype(jnp.int32), axis=1)
    chosen = jax.random.randint(jax.random.fold_in(key, 22), (TILES,), 0, 1 << 20) % (inside_count + 1)
    count_list = jnp.where(tile_ids % 7 == 3, inside_count + 1, chosen + 1).astype(jnp.int32)
    return (key_list, count_list)


def draw_key_tiles(key, part):
    return select_draw(key)[0]


def draw_tile_counts(key, part):
    return select_draw(key)[1]


def block_levels(rng, extent, shards, least, largest):
    def one(dim, shards_of):
        draws = jax.random.uniform(jax.random.fold_in(jax.random.fold_in(rng, 6), dim), (shards_of,), jnp.float32, least / len(shards), largest / len(shards))
        return jnp.repeat(jnp.exp(draws), extent[dim] // shards_of).reshape((-1,) + (1,) * (len(extent) - dim - 1))

    factor_of = one(*shards[0])
    for cut in shards[1:]:
        factor_of = factor_of * one(*cut)
    return factor_of


def centred(own_key, shape, scale, limit, pieces=(), dtype=jnp.bfloat16):
    array = jax.random.normal(own_key, shape, jnp.float32) * scale
    if len(pieces) > 0:
        array = block_levels(own_key, shape, pieces, -0.22, 0.18) * array
    return jnp.clip(array, min=-limit, max=limit).astype(dtype)


def setup_inputs(seed: int = 0, part: int = 0) -> dict:
    keys = jax.random.split(jax.random.key(seed), 9)
    part_splits = jax.random.split(jax.random.fold_in(keys[8], part), 9)
    queries = draw_queries(jax.random.fold_in(jax.random.fold_in(keys[8], part), 71), part)
    key_vectors = draw_key_vectors(jax.random.fold_in(jax.random.fold_in(keys[8], part), 71), part)
    value_vectors = centred(part_splits[2], (TOKENS, HEADS * D_HEAD), 1.0, 6.0, ((0, 16),))
    query_tangent = centred(part_splits[3], (TOKENS, HEADS * D_HEAD), 1.0, 6.0, ((0, 16),))
    key_tangent = centred(part_splits[4], (TOKENS, HEADS * D_HEAD), 1.0, 6.0, ((0, 16),))
    value_tangent = centred(part_splits[5], (TOKENS, HEADS * D_HEAD), 1.0, 6.0, ((0, 16),))
    key_tiles = draw_key_tiles(jax.random.fold_in(jax.random.fold_in(keys[8], part), 71), part)
    tile_counts = draw_tile_counts(jax.random.fold_in(jax.random.fold_in(keys[8], part), 71), part)
    return {"queries": queries, "key_vectors": key_vectors, "value_vectors": value_vectors, "query_tangent": query_tangent, "key_tangent": key_tangent, "value_tangent": value_tangent, "key_tiles": key_tiles, "tile_counts": tile_counts}


def split_heads(matrix):
    return matrix.reshape(TILES, TILE, HEADS, D_HEAD)

def reference(queries, key_vectors, value_vectors, query_tangent, key_tangent, value_tangent, key_tiles, tile_counts):
    score_scale = 1.0 / math.sqrt(D_HEAD)
    query_four = split_heads(queries)
    qtan_four = split_heads(query_tangent)
    key_four = split_heads(key_vectors)
    ktan_four = split_heads(key_tangent)
    value_four = split_heads(value_vectors)
    vtan_four = split_heads(value_tangent)

    def one_tile(index):
        chosen_ids = key_tiles[index].astype(jnp.int32)
        live_slots = jnp.arange(SEL) < tile_counts[index]
        key_mask = jnp.repeat(live_slots, TILE)

        def pick(source):
            return source[chosen_ids].reshape(SEL * TILE, HEADS, D_HEAD).astype(jnp.float32)
        query_here = query_four[index].astype(jnp.float32)
        qtan_here = qtan_four[index].astype(jnp.float32)
        keys_here = pick(key_four)
        ktan_here = pick(ktan_four)
        values_here = pick(value_four)
        vtan_here = pick(vtan_four)
        scores = jnp.einsum('qhd,khd->hqk', query_here, keys_here) * score_scale
        score_tangent = (jnp.einsum('qhd,khd->hqk', qtan_here, keys_here) + jnp.einsum('qhd,khd->hqk', query_here, ktan_here)) * score_scale
        scores = jnp.where(key_mask[None, None, :], scores, -jnp.inf)
        row_max = lax.optimization_barrier(jnp.max(scores, axis=2, keepdims=True))
        expo = jnp.exp(scores - row_max)
        total = lax.optimization_barrier(jnp.sum(expo, axis=2, keepdims=True))
        shift_mean = lax.optimization_barrier(jnp.sum(expo * score_tangent, axis=2, keepdims=True)) / total
        weights_low = lax.optimization_barrier(expo.astype(jnp.bfloat16)).astype(jnp.float32)
        tangent_low = lax.optimization_barrier((expo * (score_tangent - shift_mean)).astype(jnp.bfloat16)).astype(jnp.float32)
        primal_sum = jnp.einsum('hqk,khd->qhd', weights_low, values_here)
        tangent_sum = jnp.einsum('hqk,khd->qhd', tangent_low, values_here) + jnp.einsum('hqk,khd->qhd', weights_low, vtan_here)
        total_rows = jnp.transpose(total, (1, 0, 2))
        primal_out = (primal_sum / total_rows).astype(jnp.bfloat16).reshape(TILE, HEADS * D_HEAD)
        tangent_out = (tangent_sum / total_rows).astype(jnp.bfloat16).reshape(TILE, HEADS * D_HEAD)
        return (primal_out, tangent_out)
    primal_all, tangent_all = lax.map(one_tile, jnp.arange(TILES))
    return (primal_all.reshape(TOKENS, HEADS * D_HEAD), tangent_all.reshape(TOKENS, HEADS * D_HEAD))
```

```python
import functools
import math

import jax
import jax.numpy as jnp
from jax import lax
from jax.experimental import pallas as pl
from jax.experimental.pallas import tpu as pltpu
from jax.sharding import PartitionSpec as P

D = 128
OWN, PAIR, NEAR, FAR, CROSS = range(5)
AHEAD = 3


def kernel(
    tiles,
    q_ref,
    k_ref,
    v_ref,
    qt_ref,
    kt_ref,
    vt_ref,
    list_ref,
    count_ref,
    out_ref,
    tan_ref,
    kv,
    qq,
    res,
    load_sem,
    q_sem,
    near_send,
    near_recv,
    pair_send,
    pair_recv,
    far_send,
    far_recv,
    cross_send,
    cross_recv,
    out_sem,
):
    heads = kv.shape[1]
    slots = list_ref.shape[1]
    me = lax.axis_index("tile")
    core = me % 2
    side = (me // 2) % 2
    pair = me + 1 - 2 * core
    near = me + 2 - 4 * side
    far_to = (me + 4 - 8 * side + tiles) % tiles
    far_from = (me - 4 + 8 * side + tiles) % tiles
    lacking = NEAR + (side + core) % 2

    def columns(h):
        return pl.ds(pl.multiple_of(h * D, D), D)

    def load(h, _):
        for a, ref in enumerate((k_ref, kt_ref, v_ref, vt_ref)):
            pltpu.make_async_copy(
                ref.at[:, columns(h)], kv.at[OWN, h, :, pl.ds(a * D, D)], load_sem.at[h]
            ).start()
        for a, ref in enumerate((qt_ref, q_ref)):
            pltpu.make_async_copy(
                ref.at[:, columns(h)], qq.at[h, :, pl.ds(a * D, D)], q_sem.at[h]
            ).start()
        return 0

    lax.fori_loop(0, heads, load, 0)

    barrier = pltpu.get_barrier_semaphore()
    for other in (pair, near, far_to, far_from):
        pl.semaphore_signal(
            barrier, inc=1, device_id={"tile": other}, device_id_type=pl.DeviceIdType.MESH
        )
    pl.semaphore_wait(barrier, 4)

    def send(source, target, h, send_sem, recv_sem, other):
        return pltpu.make_async_remote_copy(
            src_ref=kv.at[source, h],
            dst_ref=kv.at[target, h],
            send_sem=send_sem.at[h],
            recv_sem=recv_sem.at[h],
            device_id={"tile": other},
            device_id_type=pl.DeviceIdType.MESH,
        )

    def to_near(h):
        return send(OWN, NEAR, h, near_send, near_recv, near)

    def to_pair(h):
        return send(OWN, PAIR, h, pair_send, pair_recv, pair)

    def to_far(h):
        return send(NEAR, FAR, h, far_send, far_recv, far_to)

    def to_cross(h):
        return send(lacking, CROSS, h, cross_send, cross_recv, pair)

    def out_copies(h):
        return [
            pltpu.make_async_copy(res.at[i, h], ref.at[:, columns(h)], out_sem.at[i, h])
            for i, ref in enumerate((out_ref, tan_ref))
        ]

    def first(h):
        pltpu.make_async_copy(kv.at[OWN, h], kv.at[OWN, h], load_sem.at[h]).wait()
        to_near(h).start()
        to_pair(h).start()

    for h in range(AHEAD):
        first(h)

    offsets = (0, 1 - 2 * core, 2 - 4 * side, 4 * side - 2, 2 * core - 1)
    biases = []
    for offset in offsets:
        chosen = jnp.int32(0)
        for slot in range(slots):
            hit = (list_ref[0, slot] == me + offset) & (slot < count_ref[0])
            chosen = jnp.where(hit, jnp.int32(1), chosen)
        biases.append(jnp.where(chosen == 1, jnp.float32(0), jnp.float32(-jnp.inf)))

    scale = 1.0 / math.sqrt(D)
    contract = functools.partial(
        lax.dot_general,
        dimension_numbers=(((1,), (1,)), ((), ())),
        preferred_element_type=jnp.float32,
    )

    def attend(h):
        both = qq[h]
        query = both[:, D:]
        scores = [
            contract(query, kv[j, h, :, 0:D]) * scale + biases[j] for j in range(5)
        ]
        tangents = [contract(both, kv[j, h, :, 0 : 2 * D]) * scale for j in range(5)]
        row_max = functools.reduce(jnp.maximum, scores).max(axis=1, keepdims=True)
        expos = [jnp.exp(s - row_max) for s in scores]
        total = functools.reduce(jnp.add, expos).sum(axis=1, keepdims=True)
        weighted = [e * t for e, t in zip(expos, tangents)]
        inverse = 1.0 / total
        mean = functools.reduce(jnp.add, weighted).sum(axis=1, keepdims=True) * inverse
        sums = jnp.zeros((both.shape[0], 2 * D), jnp.float32)
        shifted = jnp.zeros((both.shape[0], D), jnp.float32)
        for j in range(5):
            weights_low = expos[j].astype(jnp.bfloat16)
            tangent_low = (expos[j] * (tangents[j] - mean)).astype(jnp.bfloat16)
            sums += jnp.dot(
                weights_low, kv[j, h, :, 2 * D : 4 * D], preferred_element_type=jnp.float32
            )
            shifted += jnp.dot(
                tangent_low, kv[j, h, :, 2 * D : 3 * D], preferred_element_type=jnp.float32
            )
        res[0, h] = (sums[:, :D] * inverse).astype(res.dtype)
        res[1, h] = ((shifted + sums[:, D:]) * inverse).astype(res.dtype)

    def step(g, _):
        @pl.when(g < heads)
        def _():
            to_near(g).wait_recv()
            to_far(g).start()

        @pl.when(g + AHEAD < heads)
        def _():
            first(g + AHEAD)

        @pl.when(g >= 2)
        def _():
            h = g - 2
            pltpu.make_async_copy(qq.at[h], qq.at[h], q_sem.at[h]).wait()
            to_pair(h).wait_recv()
            to_cross(h).wait_recv()
            attend(h)
            for copy in out_copies(h):
                copy.start()

        @pl.when((g >= 1) & (g < heads + 1))
        def _():
            to_far(g - 1).wait_recv()
            to_cross(g - 1).start()

        return 0

    lax.fori_loop(0, heads + 2, step, 0)

    def finish(h, _):
        to_near(h).wait_send()
        to_pair(h).wait_send()
        to_far(h).wait_send()
        to_cross(h).wait_send()
        for copy in out_copies(h):
            copy.wait()
        return 0

    lax.fori_loop(0, heads, finish, 0)


def per_device(tiles, *arrays):
    queries = arrays[0]
    rows, width = queries.shape
    heads = width // D
    shape = jax.ShapeDtypeStruct(queries.shape, queries.dtype)
    anywhere = pl.BlockSpec(memory_space=pl.ANY)
    scalars = pl.BlockSpec(memory_space=pltpu.SMEM)
    per_head = pltpu.SemaphoreType.DMA((heads,))
    return pl.pallas_call(
        functools.partial(kernel, tiles),
        out_shape=(shape, shape),
        in_specs=[anywhere] * 6 + [scalars] * 2,
        out_specs=(anywhere, anywhere),
        scratch_shapes=[
            pltpu.VMEM((5, heads, rows, 4 * D), queries.dtype),
            pltpu.VMEM((heads, rows, 2 * D), queries.dtype),
            pltpu.VMEM((2, heads, rows, D), queries.dtype),
        ]
        + [per_head] * 10
        + [pltpu.SemaphoreType.DMA((2, heads))],
        compiler_params=pltpu.CompilerParams(
            collective_id=0, has_side_effects=True, vmem_limit_bytes=56 * 1024 * 1024
        ),
        cost_estimate=pl.CostEstimate(
            flops=2 * 6 * rows * rows * 5 * width,
            bytes_accessed=16 * rows * width,
            transcendentals=5 * rows * rows * heads,
        ),
    )(*arrays)


def solution(mesh):
    placed = (P(("grp", "tile"), None),) * 7 + (P(("grp", "tile")),)
    return jax.shard_map(
        functools.partial(per_device, mesh.shape["tile"]),
        mesh=mesh,
        in_specs=placed,
        out_specs=(P(("grp", "tile"), None), P(("grp", "tile"), None)),
        check_vma=False,
    )
```

```python
import functools
import math

import jax
import jax.numpy as jnp
from jax import lax
from jax.experimental import pallas as pl
from jax.experimental.pallas import tpu as pltpu
from jax.sharding import PartitionSpec as P

D = 128
OWN, PAIR, NEAR, FAR, CROSS = range(5)
PIECES = 2
AHEAD = 4
LAG = 2
UNITS = 2


def kernel(
    tiles,
    q_ref,
    k_ref,
    v_ref,
    qt_ref,
    kt_ref,
    vt_ref,
    list_ref,
    count_ref,
    out_ref,
    tan_ref,
    kv,
    qq,
    load_sem,
    q_sem,
    near_send,
    near_recv,
    pair_send,
    pair_recv,
    far_send,
    far_recv,
    cross_send,
    cross_recv,
):
    heads = kv.shape[1]
    slots = list_ref.shape[1]
    rows = kv.shape[2]
    part = rows // PIECES
    block = rows // UNITS
    pieces = heads * PIECES
    me = lax.axis_index("tile")
    core = me % 2
    side = (me // 2) % 2
    pair = me + 1 - 2 * core
    near = me + 2 - 4 * side
    far_to = (me + 4 - 8 * side + tiles) % tiles
    far_from = (me - 4 + 8 * side + tiles) % tiles
    lacking = NEAR + (side + core) % 2

    def columns(h):
        return pl.ds(pl.multiple_of(h * D, D), D)

    def load(h):
        for a, ref in enumerate((k_ref, kt_ref, v_ref, vt_ref)):
            pltpu.make_async_copy(
                ref.at[:, columns(h)], kv.at[OWN, h, :, pl.ds(a * D, D)], load_sem.at[h]
            ).start()
        for a, ref in enumerate((qt_ref, q_ref)):
            pltpu.make_async_copy(
                ref.at[:, columns(h)], qq.at[h, :, pl.ds(a * D, D)], q_sem.at[h]
            ).start()

    barrier = pltpu.get_barrier_semaphore()
    for other in (pair, near, far_to, far_from):
        pl.semaphore_signal(
            barrier, inc=1, device_id={"tile": other}, device_id_type=pl.DeviceIdType.MESH
        )
    load(0)
    load(1)
    load(2)
    pl.semaphore_wait(barrier, 4)

    def send(source, target, where, send_sem, recv_sem, other):
        return pltpu.make_async_remote_copy(
            src_ref=kv.at[(source, *where)],
            dst_ref=kv.at[(target, *where)],
            send_sem=send_sem,
            recv_sem=recv_sem,
            device_id={"tile": other},
            device_id_type=pl.DeviceIdType.MESH,
        )

    def piece(i):
        return i // PIECES, pl.ds(pl.multiple_of(i % PIECES * part, part), part)

    def to_near(i):
        return send(OWN, NEAR, piece(i), near_send.at[i], near_recv.at[i], near)

    def to_pair(h):
        return send(OWN, PAIR, (h,), pair_send.at[h], pair_recv.at[h], pair)

    def to_far(i):
        return send(NEAR, FAR, piece(i), far_send.at[i], far_recv.at[i], far_to)

    def to_cross(i):
        return send(lacking, CROSS, piece(i), cross_send.at[i], cross_recv.at[i], pair)

    def first(i):
        @pl.when(i % PIECES == 0)
        def _():
            h = i // PIECES
            pltpu.make_async_copy(kv.at[OWN, h], kv.at[OWN, h], load_sem.at[h]).wait()

        to_near(i).start()

        @pl.when(i % PIECES == 0)
        def _():
            to_pair(i // PIECES).start()

    def begin(i, _):
        first(i)
        return 0

    lax.fori_loop(0, AHEAD, begin, 0)

    offsets = (0, 1 - 2 * core, 2 - 4 * side, 4 * side - 2, 2 * core - 1)
    biases = []
    for offset in offsets:
        chosen = jnp.int32(0)
        for slot in range(slots):
            hit = (list_ref[0, slot] == me + offset) & (slot < count_ref[0])
            chosen = jnp.where(hit, jnp.int32(1), chosen)
        biases.append(jnp.where(chosen == 1, jnp.float32(0), jnp.float32(-jnp.inf)))

    scale = 1.0 / math.sqrt(D)
    contract = functools.partial(
        lax.dot_general,
        dimension_numbers=(((1,), (1,)), ((), ())),
        preferred_element_type=jnp.float32,
    )

    def attend(h, u):
        here = pl.ds(pl.multiple_of(u * block, block), block)
        both = qq[h, here, :]
        query = both[:, D:]
        scores = [
            contract(query, kv[j, h, :, 0:D]) * scale + biases[j] for j in range(5)
        ]
        tangents = [contract(both, kv[j, h, :, 0 : 2 * D]) * scale for j in range(5)]
        row_max = functools.reduce(jnp.maximum, scores).max(axis=1, keepdims=True)
        expos = [jnp.exp(s - row_max) for s in scores]
        total = functools.reduce(jnp.add, expos).sum(axis=1, keepdims=True)
        weighted = [e * t for e, t in zip(expos, tangents)]
        inverse = 1.0 / total
        mean = functools.reduce(jnp.add, weighted).sum(axis=1, keepdims=True) * inverse
        sums = jnp.zeros((both.shape[0], 2 * D), jnp.float32)
        shifted = jnp.zeros((both.shape[0], D), jnp.float32)
        for j in range(5):
            weights_low = expos[j].astype(jnp.bfloat16)
            tangent_low = (expos[j] * (tangents[j] - mean)).astype(jnp.bfloat16)
            sums += jnp.dot(
                weights_low, kv[j, h, :, 2 * D : 4 * D], preferred_element_type=jnp.float32
            )
            shifted += jnp.dot(
                tangent_low, kv[j, h, :, 2 * D : 3 * D], preferred_element_type=jnp.float32
            )
        out_ref[here, columns(h)] = (sums[:, :D] * inverse).astype(out_ref.dtype)
        tan_ref[here, columns(h)] = ((shifted + sums[:, D:]) * inverse).astype(out_ref.dtype)

    def step(g, _):
        @pl.when(g < pieces)
        def _():
            to_near(g).wait_recv()
            to_far(g).start()

        @pl.when(g + AHEAD < pieces)
        def _():
            first(g + AHEAD)

        @pl.when((g % PIECES == 1) & (g // PIECES + 3 < heads))
        def _():
            load(g // PIECES + 3)

        behind = g - (PIECES + LAG)

        @pl.when((behind >= 0) & (behind % (PIECES // UNITS) == 0))
        def _():
            h = behind // PIECES
            u = behind % PIECES // (PIECES // UNITS)

            @pl.when(u == 0)
            def _():
                pltpu.make_async_copy(qq.at[h], qq.at[h], q_sem.at[h]).wait()
                to_pair(h).wait_recv()
                for p in range(PIECES):
                    to_cross(h * PIECES + p).wait_recv()

            attend(h, u)

        @pl.when((g >= LAG) & (g < pieces + LAG))
        def _():
            to_far(g - LAG).wait_recv()
            to_cross(g - LAG).start()

        return 0

    lax.fori_loop(0, pieces + PIECES + LAG, step, 0)

    def finish(h, _):
        for p in range(PIECES):
            to_near(h * PIECES + p).wait_send()
            to_far(h * PIECES + p).wait_send()
            to_cross(h * PIECES + p).wait_send()
        to_pair(h).wait_send()
        return 0

    lax.fori_loop(0, heads, finish, 0)


def per_device(tiles, *arrays):
    queries = arrays[0]
    rows, width = queries.shape
    heads = width // D
    shape = jax.ShapeDtypeStruct(queries.shape, queries.dtype)
    anywhere = pl.BlockSpec(memory_space=pl.ANY)
    scalars = pl.BlockSpec(memory_space=pltpu.SMEM)
    per_head = pltpu.SemaphoreType.DMA((heads,))
    per_piece = pltpu.SemaphoreType.DMA((heads * PIECES,))
    kept = pltpu.VMEM(queries.shape, queries.dtype)
    whole = pl.BlockSpec(memory_space=pltpu.VMEM)
    return pl.pallas_call(
        functools.partial(kernel, tiles),
        out_shape=(kept, kept),
        in_specs=[anywhere] * 6 + [scalars] * 2,
        out_specs=(whole, whole),
        scratch_shapes=[
            pltpu.VMEM((5, heads, rows, 4 * D), queries.dtype),
            pltpu.VMEM((heads, rows, 2 * D), queries.dtype),
        ]
        + [per_head] * 2
        + [per_piece] * 2
        + [per_head] * 2
        + [per_piece] * 4,

        compiler_params=pltpu.CompilerParams(
            collective_id=0, has_side_effects=True, vmem_limit_bytes=56 * 1024 * 1024
        ),
        cost_estimate=pl.CostEstimate(
            flops=2 * 6 * rows * rows * 5 * width,
            bytes_accessed=16 * rows * width,
            transcendentals=5 * rows * rows * heads,
        ),
    )(*arrays)


def solution(mesh):
    placed = (P(("grp", "tile"), None),) * 7 + (P(("grp", "tile")),)
    return jax.shard_map(
        functools.partial(per_device, mesh.shape["tile"]),
        mesh=mesh,
        in_specs=placed,
        out_specs=(P(("grp", "tile"), None), P(("grp", "tile"), None)),
        check_vma=False,
    )
```
